32 devices in a mesh: dp: 4 (over z), ctx: 8 (over y, x, core).
Axes of the slice: x: 2, y: 2, z: 4, core: 2. Of those that a mesh axis runs over, the one named last changes fastest.
Arguments:
- hyena_q: bfloat16 [4, 1024, 4096], P('dp', 'ctx'), may hold values from -6 to 6
- hyena_k: bfloat16 [4, 1024, 4096], P('dp', 'ctx'), may hold values from -6 to 6
- hyena_v: bfloat16 [4, 1024, 4096], P('dp', 'ctx'), may hold values from -6 to 6
- hyena_cot: bfloat16 [4, 1024, 4096], P('dp', 'ctx'), may hold values from -6 to 6
- doc_lengths: int32 [4, 4], P('dp'), may hold values from 1 to 512, 1024 in all within a row
- decay_rate: float32 [16, 4096], P(None, ('dp', 'ctx')), may hold values from 0.00048828125 to 0.05
- residues: float32 [16, 4096], P(None, ('dp', 'ctx')), may hold values from -0.12 to 0.12
- skip_gain: float32 [4096], P(('dp', 'ctx')), may hold values from -3 to 3
Outputs:
- hyena_out: bfloat16 [4, 1024, 4096], P('dp', 'ctx')
- grad_hyena_q: bfloat16 [4, 1024, 4096], P('dp', 'ctx')
- grad_hyena_k: bfloat16 [4, 1024, 4096], P('dp', 'ctx')
- grad_hyena_v: bfloat16 [4, 1024, 4096], P('dp', 'ctx')
- grad_rate: float32 [16, 4096], P(None, ('dp', 'ctx'))
- grad_residues: float32 [16, 4096], P(None, ('dp', 'ctx'))
- grad_skip: float32 [4096], P(('dp', 'ctx'))
The draws below stay inside these ranges and needn't reach their ends.
Inputs may be any that keep to these rules, and one draw needn't show every extreme that they name: `doc_lengths`: each row holds the lengths of the 4 documents of one sequence in order; they sum to 1024 and the longest is exactly half of 1024.
All inputs are finite; a program needn't handle non-finite values.
Results may differ from the reference program's by a relative error of at most 0.001.
Values sent between devices are 32-bit elements; how exact they have to be, the bound alone decides.
A program may use at most 192 MiB of HBM per device.

```python
import math
import jax
import jax.numpy as jnp
import numpy as np
from jax import lax

D = 4096
MODES = 16
NDOC = 4
SEQS = 4
SEQ = 1024


def strengthened(drawn, key, source, target, blocks, factor):
    def block_of(dim):
        return (jnp.arange(drawn.shape[dim]) // (drawn.shape[dim] // blocks)).reshape((-1,) + (1,) * (drawn.ndim - 1 - dim))

    near = jax.random.permutation(key, blocks)[block_of(target)]
    far = (block_of(target) + blocks // 2) % blocks
    return jnp.where((block_of(source) == near) | (block_of(source) == far), factor * drawn, drawn)


def shard_levels(own_key, extent, shards, least, largest):
    loudness, own = 1.0, jax.random.fold_in(own_key, 6)
    for dim, shards_of in shards:
        steps = jnp.exp(jax.random.uniform(jax.random.fold_in(own, dim), (shards_of,), jnp.float32, least / len(shards), largest / len(shards)))
        loudness = loudness * jnp.repeat(steps, extent[dim] // shards_of).reshape([-1 if axis == dim else 1 for axis in range(len(extent))])
    return loudness


def profile(amount, total, most, skew):
    portions = [(1 << 20) // math.isqrt(standing ** skew) + 1 for standing in range(2, amount + 1)]
    spare, counts = total - most - (amount - 1), [1] * (amount - 1)
    while spare > 0:
        candidates = [i for i in range(amount - 1) if counts[i] < most]
        pool, remaining = sum([portions[i] for i in candidates]), spare
        for i in candidates:
            more = min(most - counts[i], max(1, remaining * portions[i] // pool), spare)
            counts[i] = counts[i] + more
            spare = spare - more
    return np.array([most] + counts)


def ragged_sizes(rng, amount, total, reach, skew):
    if amount == 2:
        one = jax.random.randint(rng, (), max(1, total - reach), min(reach, total - 1) + 1)
        return jnp.stack([one, total - one])
    sizes = jnp.asarray(profile(amount, total, reach, skew), jnp.int32)
    twos = (amount - 1) // 2
    giver, receiver = sizes[1:1 + 2 * twos:2], sizes[2:2 + 2 * twos:2]
    slack = jnp.minimum(giver - 1, reach - receiver)
    moved = jax.random.randint(jax.random.fold_in(rng, 1), (twos,), 0, 1 << 20) % (slack + 1)
    sizes = sizes.at[1:1 + 2 * twos:2].set(giver - moved).at[2:2 + 2 * twos:2].set(receiver + moved)
    return sizes[jax.random.permutation(jax.random.fold_in(rng, 2), amount)]


def bell_draw(own_key, dims, width, bound, pieces=(), kind=jnp.bfloat16):
    values = jax.random.normal(own_key, dims, jnp.float32) * width
    if len(pieces) > 0:
        values = shard_levels(own_key, dims, pieces, -0.22, 0.18) * values
    return jnp.clip(values, min=-bound, max=bound).astype(kind)


def bell_draw_with(key, extent, width, bound, shards, heavy, kind=jnp.bfloat16):
    values = width * jax.random.normal(key, extent, jnp.float32)
    if shards:
        values = values * shard_levels(key, extent, shards, -0.22, 0.18)
    return jnp.clip(strengthened(values, jax.random.fold_in(key, 3), *heavy), -bound, bound).astype(kind)


def setup_inputs(seed: int = 0) -> dict:
    key_of = jax.random.split(jax.random.key(seed), 9)
    hyena_q = bell_draw(key_of[0], (SEQS, SEQ, D), 1.0, 6.0, ((0, 4), (1, 8)))
    hyena_k = bell_draw(key_of[1], (SEQS, SEQ, D), 1.0, 6.0, ((0, 4), (1, 8)))
    hyena_v = bell_draw(key_of[2], (SEQS, SEQ, D), 1.0, 6.0, ((0, 4), (1, 8)))
    hyena_cot = bell_draw_with(key_of[3], (SEQS, SEQ, D), 1.0, 6.0, ((0, 4), (1, 8)), (1, 2, 8, 2.0))
    doc_lengths = jax.vmap(lambda own: ragged_sizes(own, NDOC, SEQ, SEQ // 2, 2))(jax.random.split(key_of[4], SEQS)).reshape((SEQS, NDOC)).astype(jnp.int32)
    decay_rate = jnp.clip(jnp.exp(math.log(0.05) - 4.6288867 * jax.random.uniform(key_of[5], (MODES, D), jnp.float32) ** shard_levels(key_of[5], (MODES, D), ((1, 32),), -0.2, 0.2)), 0.00048828125, 0.05)
    residues = bell_draw(key_of[6], (MODES, D), 0.02, 0.12, ((1, 32),), jnp.float32)
    skip_gain = bell_draw(key_of[7], (D,), 0.5, 3.0, ((0, 32),), jnp.float32)
    return dict(hyena_q=hyena_q, hyena_k=hyena_k, hyena_v=hyena_v, hyena_cot=hyena_cot, doc_lengths=doc_lengths, decay_rate=decay_rate, residues=residues, skip_gain=skip_gain)


def keep_info(lengths, total):
    ends = jnp.cumsum(lengths)
    starts = ends - lengths
    later_starts = starts[1:]
    position = jnp.arange(total, dtype=jnp.int32)
    begins = jnp.any(position[:, None] == later_starts[None, :], axis=1)
    return jnp.where(begins, 0.0, 1.0).astype(jnp.float32)


def hyena_sequence(gate_out, gate_in, filtered_in, cotangent, keep_mask, decays, residues, skip_gain):
    driven = gate_in.astype(jnp.float32) * filtered_in.astype(jnp.float32)
    pulled = cotangent.astype(jnp.float32) * gate_out.astype(jnp.float32)
    zero_state = jnp.zeros(decays.shape, jnp.float32)

    def forward_step(running, entries):
        current, sensitivity, resid_sum, decay_sum = running
        drive_row, pull_row, keep_value = entries
        new_sensitivity = keep_value * (current + decays * sensitivity)
        new_current = keep_value * decays * current + drive_row[None, :]
        filt_row = jnp.sum(residues * new_current, axis=0) + skip_gain * drive_row
        resid_sum = resid_sum + pull_row[None, :] * new_current
        decay_sum = decay_sum + pull_row[None, :] * new_sensitivity
        return (new_current, new_sensitivity, resid_sum, decay_sum), filt_row

    (_, _, resid_sum, decay_sum), filt = lax.scan(forward_step, (zero_state, zero_state, zero_state, zero_state), (driven, pulled, keep_mask))

    def reverse_step(incoming, entries):
        pull_row, keep_value = entries
        adjoint = pull_row[None, :] + incoming
        grad_row = jnp.sum(residues * adjoint, axis=0) + skip_gain * pull_row
        return keep_value * decays * adjoint, grad_row

    _, grad_drive = lax.scan(reverse_step, zero_state, (pulled, keep_mask), reverse=True)
    hyena_out = (gate_out.astype(jnp.float32) * filt).astype(jnp.bfloat16)
    grad_gate_out = (cotangent.astype(jnp.float32) * filt).astype(jnp.bfloat16)
    grad_gate_in = (grad_drive * filtered_in.astype(jnp.float32)).astype(jnp.bfloat16)
    grad_filtered = (grad_drive * gate_in.astype(jnp.float32)).astype(jnp.bfloat16)
    skip_sum = jnp.sum(pulled * driven, axis=0)
    return hyena_out, grad_gate_out, grad_gate_in, grad_filtered, resid_sum, decay_sum, skip_sum


def reference(hyena_q, hyena_k, hyena_v, hyena_cot, doc_lengths, decay_rate, residues, skip_gain):
    decays = jnp.exp(-decay_rate)

    def one_sequence(entries):
        gate_out, gate_in, filtered_in, cotangent, lengths = entries
        keep_mask = keep_info(lengths, gate_out.shape[0])
        return hyena_sequence(gate_out, gate_in, filtered_in, cotangent, keep_mask, decays, residues, skip_gain)

    results = lax.map(one_sequence, (hyena_q, hyena_k, hyena_v, hyena_cot, doc_lengths))
    hyena_out, grad_hq, grad_hk, grad_hv, resid_sums, decay_sums, skip_sums = results
    grad_residues = jnp.sum(resid_sums, axis=0)
    grad_rate = -decays * residues * jnp.sum(decay_sums, axis=0)
    grad_skip = jnp.sum(skip_sums, axis=0)
    return (hyena_out, grad_hq, grad_hk, grad_hv, grad_rate, grad_residues, grad_skip)
```

```python
import functools

import jax
import jax.numpy as jnp
from jax import lax
from jax.experimental import pallas as pl
from jax.experimental.pallas import tpu as pltpu
from jax.sharding import PartitionSpec as P

LANES = 128
ROWS = 8
GROUP = LANES * ROWS
HALF = 8
PAD = 8


def load_products(k_ref, v_ref, c_ref, q_ref, drive, pull, pitch):
    tokens = k_ref.shape[0]
    for i in range(ROWS):
        cols = pl.ds(i * LANES, LANES)
        rows = pl.ds(i * pitch, tokens)
        drive[rows, :] = k_ref[:, cols].astype(jnp.float32) * v_ref[:, cols].astype(jnp.float32)
        pull[rows, :] = c_ref[:, cols].astype(jnp.float32) * q_ref[:, cols].astype(jnp.float32)


def ends_kernel(keep_ref, flag_ref, par_ref, k_ref, v_ref, c_ref, q_ref, out_ref, drive, pull, *, modes, pitch):
    tokens = k_ref.shape[0]
    blocks = tokens // ROWS
    width = 2 * modes + 1
    base = pl.program_id(0) * ROWS * width
    load_products(k_ref, v_ref, c_ref, q_ref, drive, pull, pitch)
    lam = [jnp.exp(-par_ref[pl.ds(base + m, ROWS, stride=width), :]) for m in range(modes)]

    def steps(b, carry, masked):
        tails, heads = list(carry[0]), list(carry[1])
        for j in range(ROWS):
            t = b * ROWS + j
            u = tokens - 1 - t
            d = drive[pl.ds(t, ROWS, stride=pitch), :]
            p = pull[pl.ds(u, ROWS, stride=pitch), :]
            for m in range(modes):
                if masked:
                    tails[m] = lam[m] * keep_ref[t] * tails[m] + d
                    heads[m] = lam[m] * keep_ref[u] * (heads[m] + p)
                else:
                    tails[m] = lam[m] * tails[m] + d
                    heads[m] = lam[m] * (heads[m] + p)
        return tuple(tails), tuple(heads)

    def body(b, carry):
        broken = flag_ref[b] + flag_ref[blocks - 1 - b] > 0
        return lax.cond(broken, lambda c: steps(b, c, True), lambda c: steps(b, c, False), carry)

    zeros = tuple(jnp.zeros((ROWS, LANES), jnp.float32) for _ in range(modes))
    tails, heads = lax.fori_loop(0, blocks, body, (zeros, zeros))
    for m in range(modes):
        out_ref[m] = tails[m]
        out_ref[modes + m] = heads[m]


def main_kernel(
    keep_ref, flag_ref, par_ref, in_ref, k_ref, v_ref, c_ref, q_ref,
    out_ref, gq_ref, gk_ref, gv_ref, grad_ref,
    drive, pull, filt, gdrive, states, *, modes, pitch,
):
    tokens = k_ref.shape[0]
    blocks = tokens // ROWS
    width = 2 * modes + 1
    base = pl.program_id(0) * ROWS * width
    load_products(k_ref, v_ref, c_ref, q_ref, drive, pull, pitch)
    skip = par_ref[pl.ds(base + 2 * modes, ROWS, stride=width), :]
    skip_sum = jnp.zeros((ROWS, LANES), jnp.float32)

    for first in range(0, modes, HALF):
        lam = [jnp.exp(-par_ref[pl.ds(base + first + m, ROWS, stride=width), :]) for m in range(HALF)]
        res = [par_ref[pl.ds(base + modes + first + m, ROWS, stride=width), :] for m in range(HALF)]
        start = tuple(in_ref[first + m] for m in range(HALF))
        for m in range(HALF):
            states[0, m] = start[m]

        def forward(b, carry, masked):
            x, sums, skips = list(carry[0]), list(carry[1]), carry[2]
            for j in range(ROWS):
                t = b * ROWS + j
                here = pl.ds(t, ROWS, stride=pitch)
                d = drive[here, :]
                p = pull[here, :]
                if first == 0:
                    total = skip * d
                    skips = skips + p * d
                else:
                    total = filt[here, :]
                for m in range(HALF):
                    if masked:
                        x[m] = lam[m] * keep_ref[t] * x[m] + d
                    else:
                        x[m] = lam[m] * x[m] + d
                    states[t + 1, m] = x[m]
                    sums[m] = sums[m] + p * x[m]
                    total = total + res[m] * x[m]
                filt[here, :] = total
            return tuple(x), tuple(sums), skips

        def backward(b, carry, masked):
            inc, sums = list(carry[0]), list(carry[1])
            for j in reversed(range(ROWS)):
                t = b * ROWS + j
                here = pl.ds(t, ROWS, stride=pitch)
                p = pull[here, :]
                total = skip * p if first == 0 else gdrive[here, :]
                for m in range(HALF):
                    a = p + inc[m]
                    total = total + res[m] * a
                    inc[m] = lam[m] * keep_ref[t] * a if masked else lam[m] * a
                    sums[m] = sums[m] + inc[m] * states[t, m]
                gdrive[here, :] = total
            return tuple(inc), tuple(sums)

        def forward_body(b, carry):
            return lax.cond(
                flag_ref[b] > 0, lambda c: forward(b, c, True), lambda c: forward(b, c, False), carry
            )

        def backward_body(i, carry):
            b = blocks - 1 - i
            return lax.cond(
                flag_ref[b] > 0, lambda c: backward(b, c, True), lambda c: backward(b, c, False), carry
            )

        zeros = tuple(jnp.zeros((ROWS, LANES), jnp.float32) for _ in range(HALF))
        _, sums, skip_sum = lax.fori_loop(0, blocks, forward_body, (start, zeros, skip_sum))
        for m in range(HALF):
            grad_ref[modes + first + m] = sums[m]
        incoming = tuple(in_ref[modes + first + m] for m in range(HALF))
        _, sums = lax.fori_loop(0, blocks, backward_body, (incoming, zeros))
        for m in range(HALF):
            grad_ref[first + m] = -res[m] * sums[m]
    grad_ref[2 * modes] = skip_sum

    for i in range(ROWS):
        cols = pl.ds(i * LANES, LANES)
        rows = pl.ds(i * pitch, tokens)
        f = filt[rows, :]
        g = gdrive[rows, :]
        out_ref[:, cols] = (q_ref[:, cols].astype(jnp.float32) * f).astype(jnp.bfloat16)
        gq_ref[:, cols] = (c_ref[:, cols].astype(jnp.float32) * f).astype(jnp.bfloat16)
        gk_ref[:, cols] = (g * v_ref[:, cols].astype(jnp.float32)).astype(jnp.bfloat16)
        gv_ref[:, cols] = (g * k_ref[:, cols].astype(jnp.float32)).astype(jnp.bfloat16)


def join_kernel(weight_ref, par_ref, all_ref, out_ref, *, modes, tokens):
    count = all_ref.shape[0]
    mine = lax.axis_index("ctx")
    width = 2 * modes + 1
    base = pl.program_id(0) * ROWS * width
    for m in range(modes):
        across = jnp.exp(-float(tokens) * par_ref[pl.ds(base + m, ROWS, stride=width), :])

        def turn(i, carry):
            state, adjoint = carry
            j = count - 1 - i
            near = across * weight_ref[i] * state + all_ref[i, m]
            far = across * weight_ref[j] * adjoint + all_ref[j, modes + m]
            state = jnp.where(i < mine, near, state)
            adjoint = jnp.where(j > mine, far, adjoint)
            return state, adjoint

        zero = jnp.zeros((ROWS, LANES), jnp.float32)
        state, adjoint = lax.fori_loop(0, count, turn, (zero, zero), unroll=8)
        out_ref[m] = state
        out_ref[modes + m] = adjoint


def per_device(hyena_q, hyena_k, hyena_v, hyena_cot, doc_lengths, decay_rate, residues, skip_gain):
    tokens, channels = hyena_q.shape[1], hyena_q.shape[2]
    modes, own = decay_rate.shape
    width = 2 * modes + 1
    tiles = channels // LANES
    groups = channels // GROUP
    blocks = tokens // ROWS
    pitch = tokens + PAD
    count, mine = lax.axis_size("ctx"), lax.axis_index("ctx")
    axes = ("dp", "ctx")

    packed = jnp.concatenate([decay_rate, residues, skip_gain[None, :]], axis=0)
    params = lax.all_gather(packed, axes, axis=0)
    if own != LANES:
        params = params.transpose(1, 0, 2).reshape(width, tiles, LANES).transpose(1, 0, 2)
    params = params.reshape(tiles * width, LANES)

    lengths = doc_lengths[0]
    starts = (jnp.cumsum(lengths) - lengths)[1:]
    position = mine * tokens + jnp.arange(tokens, dtype=jnp.int32)
    starting = jnp.any(position[:, None] == starts[None, :], axis=1)
    keep = jnp.where(starting, 0.0, 1.0).astype(jnp.float32)
    flags = jnp.any(starting.reshape(blocks, ROWS), axis=1).astype(jnp.int32)
    place = jnp.arange(count)
    closed = jnp.any((starts // tokens)[None, :] == place[:, None], axis=1)
    opened = 1.0 - closed.astype(jnp.float32)
    weights = opened
    q, k, v, c = hyena_q[0], hyena_k[0], hyena_v[0], hyena_cot[0]

    smem = pl.BlockSpec(memory_space=pltpu.SMEM)
    whole = pl.BlockSpec((tiles * width, LANES), lambda g: (0, 0))
    block = pl.BlockSpec((tokens, GROUP), lambda g: (0, g))
    wide = pltpu.VMEM((ROWS * pitch, LANES), jnp.float32)
    limit = pltpu.CompilerParams(vmem_limit_bytes=48 * 1024 * 1024)

    def rows_of(n):
        return pl.BlockSpec((n, ROWS, LANES), lambda g: (0, g, 0))

    ends = pl.pallas_call(
        functools.partial(ends_kernel, modes=modes, pitch=pitch),
        grid=(groups,),
        in_specs=[smem, smem, whole, block, block, block, block],
        out_specs=rows_of(2 * modes),
        out_shape=jax.ShapeDtypeStruct((2 * modes, tiles, LANES), jnp.float32),
        scratch_shapes=[wide, wide],
        compiler_params=limit,
        name="ends",
    )(keep, flags, params, k, v, c, q)
    everyone = lax.all_gather(ends, "ctx", axis=0)
    incoming = pl.pallas_call(
        functools.partial(join_kernel, modes=modes, tokens=tokens),
        grid=(groups,),
        in_specs=[smem, whole, pl.BlockSpec((count, 2 * modes, ROWS, LANES), lambda g: (0, 0, g, 0))],
        out_specs=rows_of(2 * modes),
        out_shape=jax.ShapeDtypeStruct((2 * modes, tiles, LANES), jnp.float32),
        compiler_params=limit,
        name="join",
    )(weights, params, everyone)
    big = jax.ShapeDtypeStruct((tokens, channels), jnp.bfloat16)
    hyena_out, grad_q, grad_k, grad_v, grads = pl.pallas_call(
        functools.partial(main_kernel, modes=modes, pitch=pitch),
        grid=(groups,),
        in_specs=[smem, smem, whole, rows_of(2 * modes), block, block, block, block],
        out_specs=[block, block, block, block, rows_of(width)],
        out_shape=[big, big, big, big, jax.ShapeDtypeStruct((width, tiles, LANES), jnp.float32)],
        scratch_shapes=[wide, wide, wide, wide, pltpu.VMEM((tokens + 1, HALF, ROWS, LANES), jnp.float32)],
        compiler_params=limit,
        name="main",
    )(keep, flags, params, incoming, k, v, c, q)
    if own == LANES:
        shared = lax.psum_scatter(grads, axes, scatter_dimension=1, tiled=True).reshape(width, own)
    else:
        shared = lax.psum_scatter(grads.reshape(width, channels), axes, scatter_dimension=1, tiled=True)
    return (
        hyena_out[None], grad_q[None], grad_k[None], grad_v[None],
        shared[:modes], shared[modes : 2 * modes], shared[2 * modes],
    )


def solution(mesh):
    tokens_split = P("dp", "ctx", None)
    by_channel = P(None, ("dp", "ctx"))
    return jax.shard_map(
        per_device,
        mesh=mesh,
        in_specs=(tokens_split,) * 4 + (P("dp", None), by_channel, by_channel, P(("dp", "ctx"))),
        out_specs=(tokens_split,) * 4 + (by_channel, by_channel, P(("dp", "ctx"))),
        check_vma=False,
    )
```

```python
import functools

import jax
import jax.numpy as jnp
from jax import lax
from jax.experimental import pallas as pl
from jax.experimental.pallas import tpu as pltpu
from jax.sharding import PartitionSpec as P

LANES = 128
ROWS = 8
GROUP = LANES * ROWS
HALF = 8
PAD = 8
WIDTH = 40
VMEM_LIMIT = 56 * 1024 * 1024
MESH = pl.DeviceIdType.MESH


def tile_rows(group, row, stride):
    return pl.ds(group * (ROWS * WIDTH if stride == WIDTH else WIDTH) + row, ROWS, stride=stride)


def greet(peers):
    barrier = pltpu.get_barrier_semaphore()
    for peer in peers:
        pl.semaphore_signal(barrier, inc=1, device_id=peer, device_id_type=MESH)
    pl.semaphore_wait(barrier, len(peers))


def others(axis, size):
    mine = lax.axis_index(axis)
    return [lax.rem(mine + step, size) for step in range(1, size)]


def push(source, target, send, recv, device):
    copy = pltpu.make_async_remote_copy(
        src_ref=source, dst_ref=target, send_sem=send, recv_sem=recv, device_id=device, device_id_type=MESH
    )
    copy.start()
    return copy


def gather_kernel(own_ref, out_ref, send_z, recv_z, send_p, recv_p, *, planes, count):
    zs, ps = others("dp", planes), others("ctx", count)
    greet([{"dp": z} for z in zs] + [{"ctx": p} for p in ps])
    bundle = pl.ds(pl.multiple_of(lax.axis_index("ctx") * planes * WIDTH, WIDTH), planes * WIDTH)
    slot = pl.ds(
        pl.multiple_of((lax.axis_index("ctx") * planes + lax.axis_index("dp")) * WIDTH, WIDTH), WIDTH
    )
    copies = [push(own_ref, out_ref.at[slot], send_z.at[i], recv_z.at[i], {"dp": z}) for i, z in enumerate(zs)]
    out_ref[slot, :] = own_ref[...]
    for copy in copies:
        copy.wait()
    copies = [
        push(out_ref.at[bundle], out_ref.at[bundle], send_p.at[i], recv_p.at[i], {"ctx": p})
        for i, p in enumerate(ps)
    ]
    for copy in copies:
        copy.wait()


def exchange_kernel(open_ref, par_ref, ends_ref, out_ref, land, back, send_a, recv_a, send_b, recv_b,
                    *, planes, count, tokens):
    mine = lax.axis_index("ctx")
    ps = others("ctx", count)
    greet([{"ctx": p} for p in ps])
    copies = [
        push(ends_ref.at[p], land.at[mine], send_a.at[i], recv_a.at[i], {"ctx": p}) for i, p in enumerate(ps)
    ]
    land[mine] = ends_ref[mine]
    share = ends_ref.shape[1] // 2
    across = []
    for s in range(share):
        for g in range(planes):
            rates = par_ref[pl.ds(g * WIDTH + mine * share + s, ROWS, stride=planes * WIDTH), :]
            across.append(jnp.exp(-float(tokens) * rates))
    for copy in copies:
        copy.wait()
    for s in range(share):
        for g in range(planes):
            rows = pl.ds(g * ROWS, ROWS)
            factor = across[s * planes + g]
            state = jnp.zeros((ROWS, LANES), jnp.float32)
            adjoint = state
            for p in range(count):
                n = count - 1 - p
                back[p, s, rows, :] = state
                back[n, share + s, rows, :] = adjoint
                state = factor * open_ref[p] * state + land[p, s, rows, :]
                adjoint = factor * open_ref[n] * adjoint + land[n, share + s, rows, :]
    copies = [
        push(back.at[p], out_ref.at[mine], send_b.at[i], recv_b.at[i], {"ctx": p}) for i, p in enumerate(ps)
    ]
    out_ref[mine] = back[mine]
    for copy in copies:
        copy.wait()


def reduce_kernel(grad_ref, out_ref, land, bundle, land_z, send_p, recv_p, send_z, recv_z, *, planes, count):
    zs, ps = others("dp", planes), others("ctx", count)
    greet([{"dp": z} for z in zs] + [{"ctx": p} for p in ps])
    mine, plane = lax.axis_index("ctx"), lax.axis_index("dp")
    copies = [
        push(grad_ref.at[p], land.at[i], send_p.at[i], recv_p.at[i], {"ctx": p}) for i, p in enumerate(ps)
    ]
    for copy in copies:
        copy.wait()
    for z in range(planes):
        rows = pl.ds(z * WIDTH, WIDTH)
        total = grad_ref[mine, rows, :]
        for i in range(count - 1):
            total = total + land[i, rows, :]
        bundle[z] = total
    copies = [
        push(bundle.at[z], land_z.at[i], send_z.at[i], recv_z.at[i], {"dp": z}) for i, z in enumerate(zs)
    ]
    for copy in copies:
        copy.wait()
    total = bundle[plane]
    for i in range(planes - 1):
        total = total + land_z[i]
    out_ref[...] = total


def load_products(k_ref, v_ref, c_ref, q_ref, drive, pull, pitch):
    tokens = k_ref.shape[0]
    for i in range(ROWS):
        cols = pl.ds(i * LANES, LANES)
        rows = pl.ds(i * pitch, tokens)
        drive[rows, :] = k_ref[:, cols].astype(jnp.float32) * v_ref[:, cols].astype(jnp.float32)
        pull[rows, :] = c_ref[:, cols].astype(jnp.float32) * q_ref[:, cols].astype(jnp.float32)


def ends_kernel(keep_ref, flag_ref, par_ref, k_ref, v_ref, c_ref, q_ref, out_ref, drive, pull, *, modes, pitch, stride, share):
    tokens = k_ref.shape[0]
    blocks = tokens // ROWS
    group = pl.program_id(0)
    load_products(k_ref, v_ref, c_ref, q_ref, drive, pull, pitch)
    lam = [jnp.exp(-par_ref[tile_rows(group, m, stride), :]) for m in range(modes)]

    def steps(b, carry, masked):
        tails, heads = list(carry[0]), list(carry[1])
        for j in range(ROWS):
            t = b * ROWS + j
            u = tokens - 1 - t
            d = drive[pl.ds(t, ROWS, stride=pitch), :]
            p = pull[pl.ds(u, ROWS, stride=pitch), :]
            for m in range(modes):
                if masked:
                    tails[m] = lam[m] * keep_ref[t] * tails[m] + d
                    heads[m] = lam[m] * keep_ref[u] * (heads[m] + p)
                else:
                    tails[m] = lam[m] * tails[m] + d
                    heads[m] = lam[m] * (heads[m] + p)
        return tuple(tails), tuple(heads)

    def body(b, carry):
        broken = flag_ref[b] + flag_ref[blocks - 1 - b] > 0
        return lax.cond(broken, lambda c: steps(b, c, True), lambda c: steps(b, c, False), carry)

    zeros = tuple(jnp.zeros((ROWS, LANES), jnp.float32) for _ in range(modes))
    tails, heads = lax.fori_loop(0, blocks, body, (zeros, zeros))
    for m in range(modes):
        out_ref[m // share, m % share] = tails[m]
        out_ref[m // share, share + m % share] = heads[m]


def main_kernel(
    keep_ref, flag_ref, par_ref, in_ref, k_ref, v_ref, c_ref, q_ref,
    out_ref, gq_ref, gk_ref, gv_ref, grad_ref,
    drive, pull, filt, gdrive, states, *, modes, pitch, stride, share,
):
    tokens = k_ref.shape[0]
    blocks = tokens // ROWS
    group = pl.program_id(0)
    load_products(k_ref, v_ref, c_ref, q_ref, drive, pull, pitch)
    skip = par_ref[tile_rows(group, 2 * modes, stride), :]
    skip_sum = jnp.zeros((ROWS, LANES), jnp.float32)

    for first in range(0, modes, HALF):
        lam = [jnp.exp(-par_ref[tile_rows(group, first + m, stride), :]) for m in range(HALF)]
        res = [par_ref[tile_rows(group, modes + first + m, stride), :] for m in range(HALF)]
        start = tuple(in_ref[(first + m) // share, (first + m) % share] for m in range(HALF))
        for m in range(HALF):
            states[0, m] = start[m]

        def forward(b, carry, masked):
            x, sums, skips = list(carry[0]), list(carry[1]), carry[2]
            for j in range(ROWS):
                t = b * ROWS + j
                here = pl.ds(t, ROWS, stride=pitch)
                d = drive[here, :]
                p = pull[here, :]
                if first == 0:
                    total = skip * d
                    skips = skips + p * d
                else:
                    total = filt[here, :]
                for m in range(HALF):
                    if masked:
                        x[m] = lam[m] * keep_ref[t] * x[m] + d
                    else:
                        x[m] = lam[m] * x[m] + d
                    states[t + 1, m] = x[m]
                    sums[m] = sums[m] + p * x[m]
                    total = total + res[m] * x[m]
                filt[here, :] = total
            return tuple(x), tuple(sums), skips

        def backward(b, carry, masked):
            inc, sums = list(carry[0]), list(carry[1])
            for j in reversed(range(ROWS)):
                t = b * ROWS + j
                here = pl.ds(t, ROWS, stride=pitch)
                p = pull[here, :]
                total = skip * p if first == 0 else gdrive[here, :]
                for m in range(HALF):
                    a = p + inc[m]
                    total = total + res[m] * a
                    inc[m] = lam[m] * keep_ref[t] * a if masked else lam[m] * a
                    sums[m] = sums[m] + inc[m] * states[t, m]
                gdrive[here, :] = total
            return tuple(inc), tuple(sums)

        def forward_body(b, carry):
            return lax.cond(
                flag_ref[b] > 0, lambda c: forward(b, c, True), lambda c: forward(b, c, False), carry
            )

        def backward_body(i, carry):
            b = blocks - 1 - i
            return lax.cond(
                flag_ref[b] > 0, lambda c: backward(b, c, True), lambda c: backward(b, c, False), carry
            )

        zeros = tuple(jnp.zeros((ROWS, LANES), jnp.float32) for _ in range(HALF))
        _, sums, skip_sum = lax.fori_loop(0, blocks, forward_body, (start, zeros, skip_sum))
        for m in range(HALF):
            grad_ref[tile_rows(group, modes + first + m, stride), :] = sums[m]
        incoming = tuple(in_ref[(first + m) // share, share + (first + m) % share] for m in range(HALF))
        _, sums = lax.fori_loop(0, blocks, backward_body, (incoming, zeros))
        for m in range(HALF):
            grad_ref[tile_rows(group, first + m, stride), :] = -res[m] * sums[m]
    grad_ref[tile_rows(group, 2 * modes, stride), :] = skip_sum
    for row in range(2 * modes + 1, WIDTH):
        grad_ref[tile_rows(group, row, stride), :] = jnp.zeros((ROWS, LANES), jnp.float32)

    for i in range(ROWS):
        cols = pl.ds(i * LANES, LANES)
        rows = pl.ds(i * pitch, tokens)
        f = filt[rows, :]
        g = gdrive[rows, :]
        out_ref[:, cols] = (q_ref[:, cols].astype(jnp.float32) * f).astype(jnp.bfloat16)
        gq_ref[:, cols] = (c_ref[:, cols].astype(jnp.float32) * f).astype(jnp.bfloat16)
        gk_ref[:, cols] = (g * v_ref[:, cols].astype(jnp.float32)).astype(jnp.bfloat16)
        gv_ref[:, cols] = (g * k_ref[:, cols].astype(jnp.float32)).astype(jnp.bfloat16)


def join_kernel(weight_ref, par_ref, all_ref, out_ref, *, modes, tokens, stride, share):
    count = all_ref.shape[0]
    mine = lax.axis_index("ctx")
    group = pl.program_id(0)
    for m in range(modes):
        across = jnp.exp(-float(tokens) * par_ref[tile_rows(group, m, stride), :])

        def turn(i, carry):
            state, adjoint = carry
            j = count - 1 - i
            near = across * weight_ref[i] * state + all_ref[i, m // share, m % share]
            far = across * weight_ref[j] * adjoint + all_ref[j, m // share, share + m % share]
            state = jnp.where(i < mine, near, state)
            adjoint = jnp.where(j > mine, far, adjoint)
            return state, adjoint

        zero = jnp.zeros((ROWS, LANES), jnp.float32)
        state, adjoint = lax.fori_loop(0, count, turn, (zero, zero), unroll=8)
        out_ref[m // share, m % share] = state
        out_ref[m // share, share + m % share] = adjoint


def per_device(hyena_q, hyena_k, hyena_v, hyena_cot, doc_lengths, decay_rate, residues, skip_gain):
    tokens, channels = hyena_q.shape[1], hyena_q.shape[2]
    modes, own = decay_rate.shape
    tiles = channels // LANES
    groups = channels // GROUP
    blocks = tokens // ROWS
    pitch = tokens + PAD
    count, mine = lax.axis_size("ctx"), lax.axis_index("ctx")
    planes = lax.axis_size("dp")
    axes = ("dp", "ctx")
    direct = own == LANES and count == ROWS and modes % count == 0 and planes == groups
    stride = planes * WIDTH if direct else WIDTH
    share = modes // count if direct else 2
    tall = 2 * share
    vmem = pl.BlockSpec(memory_space=pltpu.VMEM)
    smem = pl.BlockSpec(memory_space=pltpu.SMEM)

    def remote(collective):
        return pltpu.CompilerParams(
            collective_id=collective, has_side_effects=True, vmem_limit_bytes=VMEM_LIMIT
        )

    spare = jnp.zeros((WIDTH - 2 * modes - 1, own), jnp.float32)
    packed = jnp.concatenate([decay_rate, residues, skip_gain[None, :], spare], axis=0)
    if direct:
        params = pl.pallas_call(
            functools.partial(gather_kernel, planes=planes, count=count),
            in_specs=[vmem],
            out_specs=vmem,
            out_shape=jax.ShapeDtypeStruct((tiles * WIDTH, LANES), jnp.float32),
            scratch_shapes=[pltpu.SemaphoreType.DMA((planes - 1,))] * 2
            + [pltpu.SemaphoreType.DMA((count - 1,))] * 2,
            compiler_params=remote(0),
            name="gather",
        )(packed)
    else:
        params = lax.all_gather(packed, axes, axis=1, tiled=True)
        params = params.reshape(WIDTH, tiles, LANES).transpose(1, 0, 2).reshape(tiles * WIDTH, LANES)

    lengths = doc_lengths[0]
    ends_of = [lengths[0]]
    for i in range(1, lengths.shape[0] - 1):
        ends_of.append(ends_of[-1] + lengths[i])
    starts = jnp.stack(ends_of)
    position = mine * tokens + jnp.arange(tokens, dtype=jnp.int32)
    starting = jnp.any(position[:, None] == starts[None, :], axis=1)
    keep = jnp.where(starting, 0.0, 1.0).astype(jnp.float32)
    flags = jnp.any(starting.reshape(blocks, ROWS), axis=1).astype(jnp.int32)
    place = jnp.arange(count)
    closed = jnp.any((starts // tokens)[None, :] == place[:, None], axis=1)
    opened = 1.0 - closed.astype(jnp.float32)
    q, k, v, c = hyena_q[0], hyena_k[0], hyena_v[0], hyena_cot[0]

    whole = pl.BlockSpec((tiles * WIDTH, LANES), lambda g: (0, 0))
    block = pl.BlockSpec((tokens, GROUP), lambda g: (0, g))
    wide = pltpu.VMEM((ROWS * pitch, LANES), jnp.float32)
    limit = pltpu.CompilerParams(vmem_limit_bytes=VMEM_LIMIT)

    def rows_of(n):
        return pl.BlockSpec((n // tall, tall, ROWS, LANES), lambda g: (0, 0, g, 0))

    ends = pl.pallas_call(
        functools.partial(ends_kernel, modes=modes, pitch=pitch, stride=stride, share=share),
        grid=(groups,),
        in_specs=[smem, smem, whole, block, block, block, block],
        out_specs=rows_of(2 * modes),
        out_shape=jax.ShapeDtypeStruct((2 * modes // tall, tall, tiles, LANES), jnp.float32),
        scratch_shapes=[wide, wide],
        compiler_params=limit,
        name="ends",
    )(keep, flags, params, k, v, c, q)
    if direct:
        part = pltpu.VMEM((count, tall, tiles, LANES), jnp.float32)
        incoming = pl.pallas_call(
            functools.partial(exchange_kernel, planes=planes, count=count, tokens=tokens),
            in_specs=[smem, vmem, vmem],
            out_specs=vmem,
            out_shape=jax.ShapeDtypeStruct(ends.shape, jnp.float32),
            scratch_shapes=[part, part] + [pltpu.SemaphoreType.DMA((count - 1,))] * 4,
            compiler_params=remote(1),
            name="exchange",
        )(opened, params, ends)
    else:
        everyone = lax.all_gather(ends, "ctx", axis=0)
        incoming = pl.pallas_call(
            functools.partial(join_kernel, modes=modes, tokens=tokens, stride=stride, share=share),
            grid=(groups,),
            in_specs=[
                smem, whole,
                pl.BlockSpec((count, 2 * modes // tall, tall, ROWS, LANES), lambda g: (0, 0, 0, g, 0)),
            ],
            out_specs=rows_of(2 * modes),
            out_shape=jax.ShapeDtypeStruct(ends.shape, jnp.float32),
            compiler_params=limit,
            name="join",
        )(opened, params, everyone)
    big = jax.ShapeDtypeStruct((tokens, channels), jnp.bfloat16)
    hyena_out, grad_q, grad_k, grad_v, grads = pl.pallas_call(
        functools.partial(main_kernel, modes=modes, pitch=pitch, stride=stride, share=share),
        grid=(groups,),
        in_specs=[smem, smem, whole, rows_of(2 * modes), block, block, block, block],
        out_specs=[block, block, block, block, whole],
        out_shape=[big, big, big, big, jax.ShapeDtypeStruct((tiles * WIDTH, LANES), jnp.float32)],
        scratch_shapes=[wide, wide, wide, wide, pltpu.VMEM((tokens + 1, HALF, ROWS, LANES), jnp.float32)],
        compiler_params=limit,
        name="main",
    )(keep, flags, params, incoming, k, v, c, q)
    if direct:
        chunk = planes * WIDTH
        shared = pl.pallas_call(
            functools.partial(reduce_kernel, planes=planes, count=count),
            in_specs=[vmem],
            out_specs=vmem,
            out_shape=jax.ShapeDtypeStruct((WIDTH, LANES), jnp.float32),
            scratch_shapes=[
                pltpu.VMEM((count - 1, chunk, LANES), jnp.float32),
                pltpu.VMEM((planes, WIDTH, LANES), jnp.float32),
                pltpu.VMEM((planes - 1, WIDTH, LANES), jnp.float32),
            ]
            + [pltpu.SemaphoreType.DMA((count - 1,))] * 2
            + [pltpu.SemaphoreType.DMA((planes - 1,))] * 2,
            compiler_params=remote(2),
            name="reduce",
        )(grads.reshape(count, chunk, LANES))
    else:
        grads = grads.reshape(tiles, WIDTH, LANES).transpose(1, 0, 2).reshape(WIDTH, channels)
        shared = lax.psum_scatter(grads, axes, scatter_dimension=1, tiled=True)
    return (
        hyena_out[None], grad_q[None], grad_k[None], grad_v[None],
        shared[:modes], shared[modes : 2 * modes], shared[2 * modes],
    )


def solution(mesh):
    tokens_split = P("dp", "ctx", None)
    by_channel = P(None, ("dp", "ctx"))
    return jax.shard_map(
        per_device,
        mesh=mesh,
        in_specs=(tokens_split,) * 4 + (P("dp", None), by_channel, by_channel, P(("dp", "ctx"))),
        out_specs=(tokens_split,) * 4 + (by_channel, by_channel, P(("dp", "ctx"))),
        check_vma=False,
    )
```

```python
import functools

import jax
import jax.numpy as jnp
from jax import lax
from jax.experimental import pallas as pl
from jax.experimental.pallas import tpu as pltpu
from jax.sharding import PartitionSpec as P

LANES = 128
ROWS = 8
GROUP = LANES * ROWS
HALF = 8
PAD = 8
WIDTH = 40
VMEM_LIMIT = 56 * 1024 * 1024
MESH = pl.DeviceIdType.MESH


def tile_rows(group, row, stride):
    return pl.ds(group * (ROWS * WIDTH if stride == WIDTH else WIDTH) + row, ROWS, stride=stride)


def greet(peers):
    barrier = pltpu.get_barrier_semaphore()
    for peer in peers:
        pl.semaphore_signal(barrier, inc=1, device_id=peer, device_id_type=MESH)
    pl.semaphore_wait(barrier, len(peers))


def others(axis, size):
    mine = lax.axis_index(axis)
    return [lax.rem(mine + step, size) for step in range(1, size)]


def push(source, target, send, recv, device):
    copy = pltpu.make_async_remote_copy(
        src_ref=source, dst_ref=target, send_sem=send, recv_sem=recv, device_id=device, device_id_type=MESH
    )
    copy.start()
    return copy


def chips_and_sibling(count):
    mine = lax.axis_index("ctx")
    core = lax.rem(mine, 2)
    chip = mine // 2
    chips = count // 2
    peers = [lax.rem(chip + step, chips) for step in range(1, chips)]
    return mine, core, chip, peers, mine + 1 - 2 * core


def opening(lens_ref, first, last):
    start = jnp.int32(0)
    value = jnp.float32(1.0)
    for i in range(lens_ref.shape[1] - 1):
        start = start + lens_ref[0, i]
        value = jnp.where(jnp.logical_and(start >= first, start <= last), jnp.float32(0.0), value)
    return value


def gather_kernel(rate_ref, res_ref, skip_ref, out_ref, send_z, recv_z, send_p, recv_p, send_s, recv_s,
                  *, planes, count):
    zs = others("dp", planes)
    mine, core, chip, peers, sibling = chips_and_sibling(count)
    modes = rate_ref.shape[0]
    greet([{"dp": z} for z in zs] + [{"ctx": 2 * p + core} for p in peers] + [{"ctx": sibling}])

    def bundle(device):
        return pl.ds(pl.multiple_of(device * (planes * WIDTH), WIDTH), planes * WIDTH)

    base = pl.multiple_of((mine * planes + lax.axis_index("dp")) * WIDTH, WIDTH)
    slot = pl.ds(base, WIDTH)
    out_ref[slot, :] = jnp.concatenate(
        [rate_ref[...], res_ref[...], jnp.broadcast_to(skip_ref[...], (WIDTH - 2 * modes, LANES))], axis=0
    )
    copies = [
        push(out_ref.at[slot], out_ref.at[slot], send_z.at[i], recv_z.at[i], {"dp": z}) for i, z in enumerate(zs)
    ]
    for copy in copies:
        copy.wait()
    own = out_ref.at[bundle(mine)]
    far = [push(own, own, send_p.at[i], recv_p.at[i], {"ctx": 2 * p + core}) for i, p in enumerate(peers)]
    near = [push(own, own, send_s.at[0], recv_s.at[0], {"ctx": sibling})]
    chips = len(peers) + 1
    for i, copy in enumerate(far):
        copy.wait_recv()
        got = out_ref.at[bundle(2 * lax.rem(chip + chips - 1 - i, chips) + core)]
        near.append(push(got, got, send_s.at[i + 1], recv_s.at[i + 1], {"ctx": sibling}))
    for copy in far:
        copy.wait_send()
    for copy in near:
        copy.wait()


def exchange_kernel(lens_ref, par_ref, ends_ref, out_ref, pair, total, land, back,
                    send_s, recv_s, send_p, recv_p, *, planes, count, tokens):
    mine, core, chip, peers, sibling = chips_and_sibling(count)
    greet([{"ctx": 2 * p + core} for p in peers] + [{"ctx": sibling}])
    share = ends_ref.shape[1] // 2
    chips = count // 2
    first = push(ends_ref.at[1 - core], pair, send_s.at[0], recv_s.at[0], {"ctx": sibling})
    even_open = opening(lens_ref, 2 * chip * tokens, (2 * chip + 1) * tokens - 1)
    odd_open = opening(lens_ref, (2 * chip + 1) * tokens, (2 * chip + 2) * tokens - 1)
    is_even = core == 0

    def across(m, g):
        rates = par_ref[pl.ds(g * WIDTH + core * share + m, ROWS, stride=planes * WIDTH), :]
        return jnp.exp(-float(tokens) * rates)

    def both(row, rows):
        own, other = ends_ref[core, row, rows, :], pair[row, rows, :]
        return jnp.where(is_even, own, other), jnp.where(is_even, other, own)

    first.wait()

    def join_cores(m, carry):
        for g in range(planes):
            rows = pl.ds(g * ROWS, ROWS)
            factor = across(m, g)
            even, odd = both(m, rows)
            total[0, m, rows, :] = odd + factor * odd_open * even
            even, odd = both(share + m, rows)
            total[1, m, rows, :] = even + factor * even_open * odd
        return carry

    lax.fori_loop(0, share, join_cores, 0)
    copies = [
        push(total.at[jnp.where(p > chip, 0, 1)], land.at[chip], send_p.at[i], recv_p.at[i], {"ctx": 2 * p + core})
        for i, p in enumerate(peers)
    ]
    land[chip] = jnp.zeros(land.shape[1:], jnp.float32)
    opened = [opening(lens_ref, 2 * r * tokens, (2 * r + 2) * tokens - 1) for r in range(chips)]
    for copy in copies:
        copy.wait()

    def enter(m, carry):
        for g in range(planes):
            rows = pl.ds(g * ROWS, ROWS)
            factor = across(m, g)
            square = factor * factor
            state = jnp.zeros((ROWS, LANES), jnp.float32)
            adjoint = state
            for r in range(chips):
                n = chips - 1 - r
                state = jnp.where(r < chip, square * opened[r] * state + land[r, m, rows, :], state)
                adjoint = jnp.where(n > chip, square * opened[n] * adjoint + land[n, m, rows, :], adjoint)
            even_tail, _ = both(m, rows)
            _, odd_head = both(share + m, rows)
            odd_state = even_tail + factor * even_open * state
            even_adjoint = odd_head + factor * odd_open * adjoint
            out_ref[core, m, rows, :] = jnp.where(is_even, state, odd_state)
            out_ref[core, share + m, rows, :] = jnp.where(is_even, even_adjoint, adjoint)
            back[m, rows, :] = jnp.where(is_even, odd_state, state)
            back[share + m, rows, :] = jnp.where(is_even, adjoint, even_adjoint)
        return carry

    lax.fori_loop(0, share, enter, 0)
    push(back, out_ref.at[core], send_s.at[1], recv_s.at[1], {"ctx": sibling}).wait()


def reduce_kernel(grad_ref, rate_ref, res_ref, skip_ref, pair, stage, land, bundle, land_z,
                  send_s, recv_s, send_p, recv_p, send_z, recv_z, *, planes, count):
    zs = others("dp", planes)
    mine, core, chip, peers, sibling = chips_and_sibling(count)
    plane = lax.axis_index("dp")
    greet([{"dp": z} for z in zs] + [{"ctx": 2 * p + core} for p in peers] + [{"ctx": sibling}])
    order = peers + [chip]
    near = [
        push(grad_ref.at[2 * p + 1 - core], pair.at[i], send_s.at[i], recv_s.at[i], {"ctx": sibling})
        for i, p in enumerate(order)
    ]
    far = []
    for i, p in enumerate(peers):
        near[i].wait_recv()
        stage[i] = grad_ref[2 * p + core] + pair[i]
        far.append(push(stage.at[i], land.at[i], send_p.at[i], recv_p.at[i], {"ctx": 2 * p + core}))
    last = len(peers)
    near[last].wait_recv()
    for copy in near:
        copy.wait_send()
    for copy in far:
        copy.wait()
    for z in range(planes):
        rows = pl.ds(z * WIDTH, WIDTH)
        total = grad_ref[mine, rows, :] + pair[last, rows, :]
        for i in range(last):
            total = total + land[i, rows, :]
        bundle[z] = total
    copies = [
        push(bundle.at[z], land_z.at[i], send_z.at[i], recv_z.at[i], {"dp": z}) for i, z in enumerate(zs)
    ]
    for copy in copies:
        copy.wait()
    total = bundle[plane]
    for i in range(planes - 1):
        total = total + land_z[i]
    modes = rate_ref.shape[0]
    rate_ref[...] = total[:modes]
    res_ref[...] = total[modes : 2 * modes]
    skip_ref[...] = total[2 * modes : 2 * modes + 1]


def load_products(k_ref, v_ref, c_ref, q_ref, drive, pull, pitch):
    tokens = k_ref.shape[0]
    for i in range(ROWS):
        cols = pl.ds(i * LANES, LANES)
        rows = pl.ds(i * pitch, tokens)
        drive[rows, :] = k_ref[:, cols].astype(jnp.float32) * v_ref[:, cols].astype(jnp.float32)
        pull[rows, :] = c_ref[:, cols].astype(jnp.float32) * q_ref[:, cols].astype(jnp.float32)


def ends_kernel(lens_ref, par_ref, k_ref, v_ref, c_ref, q_ref, out_ref, drive, pull, *, modes, pitch, stride, share):
    tokens = k_ref.shape[0]
    blocks = tokens // ROWS
    group = pl.program_id(0)
    origin = lax.axis_index("ctx") * tokens

    def keep(t):
        return opening(lens_ref, origin + t, origin + t)

    def broken(b):
        return opening(lens_ref, origin + b * ROWS, origin + b * ROWS + ROWS - 1) < 0.5

    load_products(k_ref, v_ref, c_ref, q_ref, drive, pull, pitch)
    lam = [jnp.exp(-par_ref[tile_rows(group, m, stride), :]) for m in range(modes)]

    def steps(b, carry, masked):
        tails, heads = list(carry[0]), list(carry[1])
        for j in range(ROWS):
            t = b * ROWS + j
            u = tokens - 1 - t
            d = drive[pl.ds(t, ROWS, stride=pitch), :]
            p = pull[pl.ds(u, ROWS, stride=pitch), :]
            for m in range(modes):
                if masked:
                    tails[m] = lam[m] * keep(t) * tails[m] + d
                    heads[m] = lam[m] * keep(u) * (heads[m] + p)
                else:
                    tails[m] = lam[m] * tails[m] + d
                    heads[m] = lam[m] * (heads[m] + p)
        return tuple(tails), tuple(heads)

    def body(b, carry):
        either = jnp.logical_or(broken(b), broken(blocks - 1 - b))
        return lax.cond(either, lambda c: steps(b, c, True), lambda c: steps(b, c, False), carry)

    zeros = tuple(jnp.zeros((ROWS, LANES), jnp.float32) for _ in range(modes))
    tails, heads = lax.fori_loop(0, blocks, body, (zeros, zeros))
    for m in range(modes):
        out_ref[m // share, m % share] = tails[m]
        out_ref[m // share, share + m % share] = heads[m]


def main_kernel(
    lens_ref, par_ref, in_ref, k_ref, v_ref, c_ref, q_ref,
    out_ref, gq_ref, gk_ref, gv_ref, grad_ref,
    drive, pull, filt, gdrive, states, *, modes, pitch, stride, share,
):
    tokens = k_ref.shape[0]
    blocks = tokens // ROWS
    group = pl.program_id(0)
    origin = lax.axis_index("ctx") * tokens

    def keep(t):
        return opening(lens_ref, origin + t, origin + t)

    def broken(b):
        return opening(lens_ref, origin + b * ROWS, origin + b * ROWS + ROWS - 1) < 0.5

    load_products(k_ref, v_ref, c_ref, q_ref, drive, pull, pitch)
    skip = par_ref[tile_rows(group, 2 * modes, stride), :]
    skip_sum = jnp.zeros((ROWS, LANES), jnp.float32)

    for first in range(0, modes, HALF):
        lam = [jnp.exp(-par_ref[tile_rows(group, first + m, stride), :]) for m in range(HALF)]
        res = [par_ref[tile_rows(group, modes + first + m, stride), :] for m in range(HALF)]
        start = tuple(in_ref[(first + m) // share, (first + m) % share] for m in range(HALF))
        for m in range(HALF):
            states[0, m] = start[m]

        def forward(b, carry, masked):
            x, sums, skips = list(carry[0]), list(carry[1]), carry[2]
            for j in range(ROWS):
                t = b * ROWS + j
                here = pl.ds(t, ROWS, stride=pitch)
                d = drive[here, :]
                p = pull[here, :]
                if first == 0:
                    total = skip * d
                    skips = skips + p * d
                else:
                    total = filt[here, :]
                for m in range(HALF):
                    if masked:
                        x[m] = lam[m] * keep(t) * x[m] + d
                    else:
                        x[m] = lam[m] * x[m] + d
                    states[t + 1, m] = x[m]
                    sums[m] = sums[m] + p * x[m]
                    total = total + res[m] * x[m]
                filt[here, :] = total
            return tuple(x), tuple(sums), skips

        def backward(b, carry, masked):
            inc, sums = list(carry[0]), list(carry[1])
            for j in reversed(range(ROWS)):
                t = b * ROWS + j
                here = pl.ds(t, ROWS, stride=pitch)
                p = pull[here, :]
                total = skip * p if first == 0 else gdrive[here, :]
                for m in range(HALF):
                    a = p + inc[m]
                    total = total + res[m] * a
                    inc[m] = lam[m] * keep(t) * a if masked else lam[m] * a
                    sums[m] = sums[m] + inc[m] * states[t, m]
                gdrive[here, :] = total
            return tuple(inc), tuple(sums)

        def forward_body(b, carry):
            return lax.cond(
                broken(b), lambda c: forward(b, c, True), lambda c: forward(b, c, False), carry
            )

        def backward_body(i, carry):
            b = blocks - 1 - i
            return lax.cond(
                broken(b), lambda c: backward(b, c, True), lambda c: backward(b, c, False), carry
            )

        zeros = tuple(jnp.zeros((ROWS, LANES), jnp.float32) for _ in range(HALF))
        _, sums, skip_sum = lax.fori_loop(0, blocks, forward_body, (start, zeros, skip_sum))
        for m in range(HALF):
            grad_ref[tile_rows(group, modes + first + m, stride), :] = sums[m]
        incoming = tuple(in_ref[(first + m) // share, share + (first + m) % share] for m in range(HALF))
        _, sums = lax.fori_loop(0, blocks, backward_body, (incoming, zeros))
        for m in range(HALF):
            grad_ref[tile_rows(group, first + m, stride), :] = -res[m] * sums[m]
    grad_ref[tile_rows(group, 2 * modes, stride), :] = skip_sum
    for row in range(2 * modes + 1, WIDTH):
        grad_ref[tile_rows(group, row, stride), :] = jnp.zeros((ROWS, LANES), jnp.float32)

    for i in range(ROWS):
        cols = pl.ds(i * LANES, LANES)
        rows = pl.ds(i * pitch, tokens)
        f = filt[rows, :]
        g = gdrive[rows, :]
        out_ref[:, cols] = (q_ref[:, cols].astype(jnp.float32) * f).astype(jnp.bfloat16)
        gq_ref[:, cols] = (c_ref[:, cols].astype(jnp.float32) * f).astype(jnp.bfloat16)
        gk_ref[:, cols] = (g * v_ref[:, cols].astype(jnp.float32)).astype(jnp.bfloat16)
        gv_ref[:, cols] = (g * k_ref[:, cols].astype(jnp.float32)).astype(jnp.bfloat16)


def join_kernel(lens_ref, par_ref, all_ref, out_ref, *, modes, tokens, stride, share):
    count = all_ref.shape[0]
    mine = lax.axis_index("ctx")
    group = pl.program_id(0)
    for m in range(modes):
        across = jnp.exp(-float(tokens) * par_ref[tile_rows(group, m, stride), :])

        def turn(i, carry):
            state, adjoint = carry
            j = count - 1 - i
            near = across * opening(lens_ref, i * tokens, (i + 1) * tokens - 1) * state + all_ref[i, m // share, m % share]
            far = across * opening(lens_ref, j * tokens, (j + 1) * tokens - 1) * adjoint + all_ref[j, m // share, share + m % share]
            state = jnp.where(i < mine, near, state)
            adjoint = jnp.where(j > mine, far, adjoint)
            return state, adjoint

        zero = jnp.zeros((ROWS, LANES), jnp.float32)
        state, adjoint = lax.fori_loop(0, count, turn, (zero, zero), unroll=8)
        out_ref[m // share, m % share] = state
        out_ref[m // share, share + m % share] = adjoint


def per_device(hyena_q, hyena_k, hyena_v, hyena_cot, doc_lengths, decay_rate, residues, skip_gain):
    tokens, channels = hyena_q.shape[1], hyena_q.shape[2]
    modes, own = decay_rate.shape
    tiles = channels // LANES
    groups = channels // GROUP
    pitch = tokens + PAD
    count = lax.axis_size("ctx")
    planes = lax.axis_size("dp")
    axes = ("dp", "ctx")
    direct = own == LANES and count == ROWS and modes % 2 == 0 and planes == groups
    stride = planes * WIDTH if direct else WIDTH
    share = modes // 2
    tall = 2 * share
    vmem = pl.BlockSpec(memory_space=pltpu.VMEM)
    smem = pl.BlockSpec(memory_space=pltpu.SMEM)

    def remote(collective):
        return pltpu.CompilerParams(
            collective_id=collective, has_side_effects=True, vmem_limit_bytes=VMEM_LIMIT
        )

    if direct:
        params = pl.pallas_call(
            functools.partial(gather_kernel, planes=planes, count=count),
            in_specs=[vmem, vmem, vmem],
            out_specs=vmem,
            out_shape=jax.ShapeDtypeStruct((tiles * WIDTH, LANES), jnp.float32),
            scratch_shapes=[pltpu.SemaphoreType.DMA((planes - 1,))] * 2
            + [pltpu.SemaphoreType.DMA((count // 2 - 1,))] * 2
            + [pltpu.SemaphoreType.DMA((count // 2,))] * 2,
            compiler_params=remote(0),
            name="gather",
        )(decay_rate, residues, skip_gain[None, :])
    else:
        spare = jnp.zeros((WIDTH - 2 * modes - 1, own), jnp.float32)
        packed = jnp.concatenate([decay_rate, residues, skip_gain[None, :], spare], axis=0)
        params = lax.all_gather(packed, axes, axis=1, tiled=True)
        params = params.reshape(WIDTH, tiles, LANES).transpose(1, 0, 2).reshape(tiles * WIDTH, LANES)

    q, k, v, c = hyena_q[0], hyena_k[0], hyena_v[0], hyena_cot[0]

    whole = pl.BlockSpec((tiles * WIDTH, LANES), lambda g: (0, 0))
    block = pl.BlockSpec((tokens, GROUP), lambda g: (0, g))
    wide = pltpu.VMEM((ROWS * pitch, LANES), jnp.float32)
    limit = pltpu.CompilerParams(vmem_limit_bytes=VMEM_LIMIT)

    def rows_of(n):
        return pl.BlockSpec((n // tall, tall, ROWS, LANES), lambda g: (0, 0, g, 0))

    ends = pl.pallas_call(
        functools.partial(ends_kernel, modes=modes, pitch=pitch, stride=stride, share=share),
        grid=(groups,),
        in_specs=[smem, whole, block, block, block, block],
        out_specs=rows_of(2 * modes),
        out_shape=jax.ShapeDtypeStruct((2 * modes // tall, tall, tiles, LANES), jnp.float32),
        scratch_shapes=[wide, wide],
        compiler_params=limit,
        name="ends",
    )(doc_lengths, params, k, v, c, q)
    if direct:
        part = pltpu.VMEM((tall, tiles, LANES), jnp.float32)
        chips = count // 2
        incoming = pl.pallas_call(
            functools.partial(exchange_kernel, planes=planes, count=count, tokens=tokens),
            in_specs=[smem, vmem, vmem],
            out_specs=vmem,
            out_shape=jax.ShapeDtypeStruct(ends.shape, jnp.float32),
            scratch_shapes=[
                part,
                pltpu.VMEM((2, share, tiles, LANES), jnp.float32),
                pltpu.VMEM((chips, share, tiles, LANES), jnp.float32),
                part,
            ]
            + [pltpu.SemaphoreType.DMA((2,))] * 2
            + [pltpu.SemaphoreType.DMA((chips - 1,))] * 2,
            compiler_params=remote(1),
            name="exchange",
        )(doc_lengths, params, ends)
    else:
        everyone = lax.all_gather(ends, "ctx", axis=0)
        incoming = pl.pallas_call(
            functools.partial(join_kernel, modes=modes, tokens=tokens, stride=stride, share=share),
            grid=(groups,),
            in_specs=[
                smem, whole,
                pl.BlockSpec((count, 2 * modes // tall, tall, ROWS, LANES), lambda g: (0, 0, 0, g, 0)),
            ],
            out_specs=rows_of(2 * modes),
            out_shape=jax.ShapeDtypeStruct(ends.shape, jnp.float32),
            compiler_params=limit,
            name="join",
        )(doc_lengths, params, everyone)
    big = jax.ShapeDtypeStruct((tokens, channels), jnp.bfloat16)
    hyena_out, grad_q, grad_k, grad_v, grads = pl.pallas_call(
        functools.partial(main_kernel, modes=modes, pitch=pitch, stride=stride, share=share),
        grid=(groups,),
        in_specs=[smem, whole, rows_of(2 * modes), block, block, block, block],
        out_specs=[block, block, block, block, whole],
        out_shape=[big, big, big, big, jax.ShapeDtypeStruct((tiles * WIDTH, LANES), jnp.float32)],
        scratch_shapes=[wide, wide, wide, wide, pltpu.VMEM((tokens + 1, HALF, ROWS, LANES), jnp.float32)],
        compiler_params=limit,
        name="main",
    )(doc_lengths, params, incoming, k, v, c, q)
    if direct:
        chunk = planes * WIDTH
        row = jax.ShapeDtypeStruct((modes, LANES), jnp.float32)
        grad_rate, grad_residues, grad_skip = pl.pallas_call(
            functools.partial(reduce_kernel, planes=planes, count=count),
            in_specs=[vmem],
            out_specs=[vmem, vmem, vmem],
            out_shape=[row, row, jax.ShapeDtypeStruct((1, LANES), jnp.float32)],
            scratch_shapes=[
                pltpu.VMEM((chips, chunk, LANES), jnp.float32),
                pltpu.VMEM((chips - 1, chunk, LANES), jnp.float32),
                pltpu.VMEM((chips - 1, chunk, LANES), jnp.float32),
                pltpu.VMEM((planes, WIDTH, LANES), jnp.float32),
                pltpu.VMEM((planes - 1, WIDTH, LANES), jnp.float32),
            ]
            + [pltpu.SemaphoreType.DMA((chips,))] * 2
            + [pltpu.SemaphoreType.DMA((chips - 1,))] * 2
            + [pltpu.SemaphoreType.DMA((planes - 1,))] * 2,
            compiler_params=remote(2),
            name="reduce",
        )(grads.reshape(count, chunk, LANES))
        grad_skip = grad_skip[0]
    else:
        grads = grads.reshape(tiles, WIDTH, LANES).transpose(1, 0, 2).reshape(WIDTH, channels)
        shared = lax.psum_scatter(grads, axes, scatter_dimension=1, tiled=True)
        grad_rate, grad_residues, grad_skip = shared[:modes], shared[modes : 2 * modes], shared[2 * modes]
    return (
        hyena_out[None], grad_q[None], grad_k[None], grad_v[None],
        grad_rate, grad_residues, grad_skip,
    )


def solution(mesh):
    tokens_split = P("dp", "ctx", None)
    by_channel = P(None, ("dp", "ctx"))
    return jax.shard_map(
        per_device,
        mesh=mesh,
        in_specs=(tokens_split,) * 4 + (P("dp", None), by_channel, by_channel, P(("dp", "ctx"))),
        out_specs=(tokens_split,) * 4 + (by_channel, by_channel, P(("dp", "ctx"))),
        check_vma=False,
    )
```

```python
import functools

import jax
import jax.numpy as jnp
from jax import lax
from jax.experimental import pallas as pl
from jax.experimental.pallas import tpu as pltpu
from jax.sharding import PartitionSpec as P

LANES = 128
ROWS = 8
STEP = 16
GROUP = LANES * ROWS
HALF = 8
PAD = 8
WIDTH = 40
VMEM_LIMIT = 56 * 1024 * 1024
MESH = pl.DeviceIdType.MESH


def tile_rows(group, row, stride):
    return pl.ds(group * (ROWS * WIDTH if stride == WIDTH else WIDTH) + row, ROWS, stride=stride)


def greet(peers):
    barrier = pltpu.get_barrier_semaphore()
    for peer in peers:
        pl.semaphore_signal(barrier, inc=1, device_id=peer, device_id_type=MESH)
    pl.semaphore_wait(barrier, len(peers))


def others(axis, size):
    mine = lax.axis_index(axis)
    return [lax.rem(mine + step, size) for step in range(1, size)]


def push(source, target, send, recv, device):
    copy = pltpu.make_async_remote_copy(
        src_ref=source, dst_ref=target, send_sem=send, recv_sem=recv, device_id=device, device_id_type=MESH
    )
    copy.start()
    return copy


def chips_and_sibling(count):
    mine = lax.axis_index("ctx")
    core = lax.rem(mine, 2)
    chip = mine // 2
    chips = count // 2
    peers = [lax.rem(chip + step, chips) for step in range(1, chips)]
    return mine, core, chip, peers, mine + 1 - 2 * core


def opening(lens_ref, first, last):
    start = jnp.int32(0)
    value = jnp.float32(1.0)
    for i in range(lens_ref.shape[1] - 1):
        start = start + lens_ref[0, i]
        value = jnp.where(jnp.logical_and(start >= first, start <= last), jnp.float32(0.0), value)
    return value


def gather_kernel(rate_ref, res_ref, skip_ref, out_ref, send_z, recv_z, send_p, recv_p, send_s, recv_s,
                  *, planes, count):
    zs = others("dp", planes)
    mine, core, chip, peers, sibling = chips_and_sibling(count)
    modes = rate_ref.shape[0]
    greet([{"dp": z} for z in zs] + [{"ctx": 2 * p + core} for p in peers] + [{"ctx": sibling}])

    def bundle(device):
        return pl.ds(pl.multiple_of(device * (planes * WIDTH), WIDTH), planes * WIDTH)

    base = pl.multiple_of((mine * planes + lax.axis_index("dp")) * WIDTH, WIDTH)
    slot = pl.ds(base, WIDTH)
    out_ref[slot, :] = jnp.concatenate(
        [rate_ref[...], res_ref[...], jnp.broadcast_to(skip_ref[...], (WIDTH - 2 * modes, LANES))], axis=0
    )
    copies = [
        push(out_ref.at[slot], out_ref.at[slot], send_z.at[i], recv_z.at[i], {"dp": z}) for i, z in enumerate(zs)
    ]
    for copy in copies:
        copy.wait()
    own = out_ref.at[bundle(mine)]
    far = [push(own, own, send_p.at[i], recv_p.at[i], {"ctx": 2 * p + core}) for i, p in enumerate(peers)]
    near = [push(own, own, send_s.at[0], recv_s.at[0], {"ctx": sibling})]
    chips = len(peers) + 1
    for i, copy in enumerate(far):
        copy.wait_recv()
        got = out_ref.at[bundle(2 * lax.rem(chip + chips - 1 - i, chips) + core)]
        near.append(push(got, got, send_s.at[i + 1], recv_s.at[i + 1], {"ctx": sibling}))
    for copy in far:
        copy.wait_send()
    for copy in near:
        copy.wait()


def exchange_kernel(lens_ref, par_ref, ends_ref, out_ref, pair, total, land, back,
                    send_s, recv_s, send_p, recv_p, *, planes, count, tokens):
    mine, core, chip, peers, sibling = chips_and_sibling(count)
    greet([{"ctx": 2 * p + core} for p in peers] + [{"ctx": sibling}])
    share = ends_ref.shape[1] // 2
    chips = count // 2
    first = push(ends_ref.at[1 - core], pair, send_s.at[0], recv_s.at[0], {"ctx": sibling})
    even_open = opening(lens_ref, 2 * chip * tokens, (2 * chip + 1) * tokens - 1)
    odd_open = opening(lens_ref, (2 * chip + 1) * tokens, (2 * chip + 2) * tokens - 1)
    is_even = core == 0

    def across(m, g):
        rates = par_ref[pl.ds(g * WIDTH + core * share + m, ROWS, stride=planes * WIDTH), :]
        return jnp.exp(-float(tokens) * rates)

    def both(row, rows):
        own, other = ends_ref[core, row, rows, :], pair[row, rows, :]
        return jnp.where(is_even, own, other), jnp.where(is_even, other, own)

    first.wait()

    def join_cores(m, carry):
        for g in range(planes):
            rows = pl.ds(g * ROWS, ROWS)
            factor = across(m, g)
            even, odd = both(m, rows)
            total[0, m, rows, :] = odd + factor * odd_open * even
            even, odd = both(share + m, rows)
            total[1, m, rows, :] = even + factor * even_open * odd
        return carry

    lax.fori_loop(0, share, join_cores, 0)
    copies = [
        push(total.at[jnp.where(p > chip, 0, 1)], land.at[chip], send_p.at[i], recv_p.at[i], {"ctx": 2 * p + core})
        for i, p in enumerate(peers)
    ]
    land[chip] = jnp.zeros(land.shape[1:], jnp.float32)
    opened = [opening(lens_ref, 2 * r * tokens, (2 * r + 2) * tokens - 1) for r in range(chips)]
    for copy in copies:
        copy.wait()

    def enter(m, carry):
        for g in range(planes):
            rows = pl.ds(g * ROWS, ROWS)
            factor = across(m, g)
            square = factor * factor
            state = jnp.zeros((ROWS, LANES), jnp.float32)
            adjoint = state
            for r in range(chips):
                n = chips - 1 - r
                state = jnp.where(r < chip, square * opened[r] * state + land[r, m, rows, :], state)
                adjoint = jnp.where(n > chip, square * opened[n] * adjoint + land[n, m, rows, :], adjoint)
            even_tail, _ = both(m, rows)
            _, odd_head = both(share + m, rows)
            odd_state = even_tail + factor * even_open * state
            even_adjoint = odd_head + factor * odd_open * adjoint
            out_ref[core, m, rows, :] = jnp.where(is_even, state, odd_state)
            out_ref[core, share + m, rows, :] = jnp.where(is_even, even_adjoint, adjoint)
            back[m, rows, :] = jnp.where(is_even, odd_state, state)
            back[share + m, rows, :] = jnp.where(is_even, adjoint, even_adjoint)
        return carry

    lax.fori_loop(0, share, enter, 0)
    push(back, out_ref.at[core], send_s.at[1], recv_s.at[1], {"ctx": sibling}).wait()


def reduce_kernel(grad_ref, rate_ref, res_ref, skip_ref, pair, stage, land, bundle, land_z,
                  send_s, recv_s, send_p, recv_p, send_z, recv_z, *, planes, count):
    zs = others("dp", planes)
    mine, core, chip, peers, sibling = chips_and_sibling(count)
    plane = lax.axis_index("dp")
    greet([{"dp": z} for z in zs] + [{"ctx": 2 * p + core} for p in peers] + [{"ctx": sibling}])
    order = peers + [chip]
    near = [
        push(grad_ref.at[2 * p + 1 - core], pair.at[i], send_s.at[i], recv_s.at[i], {"ctx": sibling})
        for i, p in enumerate(order)
    ]
    far = []
    for i, p in enumerate(peers):
        near[i].wait_recv()
        stage[i] = grad_ref[2 * p + core] + pair[i]
        far.append(push(stage.at[i], land.at[i], send_p.at[i], recv_p.at[i], {"ctx": 2 * p + core}))
    last = len(peers)
    near[last].wait_recv()
    for copy in near:
        copy.wait_send()
    for copy in far:
        copy.wait()
    for z in range(planes):
        rows = pl.ds(z * WIDTH, WIDTH)
        total = grad_ref[mine, rows, :] + pair[last, rows, :]
        for i in range(last):
            total = total + land[i, rows, :]
        bundle[z] = total
    copies = [
        push(bundle.at[z], land_z.at[i], send_z.at[i], recv_z.at[i], {"dp": z}) for i, z in enumerate(zs)
    ]
    for copy in copies:
        copy.wait()
    total = bundle[plane]
    for i in range(planes - 1):
        total = total + land_z[i]
    modes = rate_ref.shape[0]
    rate_ref[...] = total[:modes]
    res_ref[...] = total[modes : 2 * modes]
    skip_ref[...] = total[2 * modes : 2 * modes + 1]


def load_products(k_ref, v_ref, c_ref, q_ref, drive, pull, pitch):
    tokens = k_ref.shape[0]
    for i in range(ROWS):
        cols = pl.ds(i * LANES, LANES)
        rows = pl.ds(i * pitch, tokens)
        drive[rows, :] = k_ref[:, cols].astype(jnp.float32) * v_ref[:, cols].astype(jnp.float32)
        pull[rows, :] = c_ref[:, cols].astype(jnp.float32) * q_ref[:, cols].astype(jnp.float32)


def ends_kernel(lens_ref, par_ref, k_ref, v_ref, c_ref, q_ref, out_ref, drive, pull, *, modes, pitch, stride, share):
    tokens = k_ref.shape[0]
    blocks = tokens // STEP
    group = pl.program_id(0)
    origin = lax.axis_index("ctx") * tokens

    def keep(t):
        return opening(lens_ref, origin + t, origin + t)

    def broken(b):
        return opening(lens_ref, origin + b * STEP, origin + b * STEP + STEP - 1) < 0.5

    load_products(k_ref, v_ref, c_ref, q_ref, drive, pull, pitch)
    lam = [jnp.exp(-par_ref[tile_rows(group, m, stride), :]) for m in range(modes)]

    def steps(b, carry, masked):
        tails, heads = list(carry[0]), list(carry[1])
        for j in range(STEP):
            t = b * STEP + j
            u = tokens - 1 - t
            d = drive[pl.ds(t, ROWS, stride=pitch), :]
            p = pull[pl.ds(u, ROWS, stride=pitch), :]
            for m in range(modes):
                if masked:
                    tails[m] = lam[m] * keep(t) * tails[m] + d
                    heads[m] = lam[m] * keep(u) * (heads[m] + p)
                else:
                    tails[m] = lam[m] * tails[m] + d
                    heads[m] = lam[m] * (heads[m] + p)
        return tuple(tails), tuple(heads)

    def body(b, carry):
        either = jnp.logical_or(broken(b), broken(blocks - 1 - b))
        return lax.cond(either, lambda c: steps(b, c, True), lambda c: steps(b, c, False), carry)

    zeros = tuple(jnp.zeros((ROWS, LANES), jnp.float32) for _ in range(modes))
    tails, heads = lax.fori_loop(0, blocks, body, (zeros, zeros))
    for m in range(modes):
        out_ref[m // share, m % share] = tails[m]
        out_ref[m // share, share + m % share] = heads[m]


def main_kernel(
    lens_ref, par_ref, in_ref, k_ref, v_ref, c_ref, q_ref,
    out_ref, gq_ref, gk_ref, gv_ref, grad_ref,
    drive, pull, filt, gdrive, states, *, modes, pitch, stride, share,
):
    tokens = k_ref.shape[0]
    blocks = tokens // STEP
    group = pl.program_id(0)
    origin = lax.axis_index("ctx") * tokens

    def keep(t):
        return opening(lens_ref, origin + t, origin + t)

    def broken(b):
        return opening(lens_ref, origin + b * STEP, origin + b * STEP + STEP - 1) < 0.5

    load_products(k_ref, v_ref, c_ref, q_ref, drive, pull, pitch)
    skip = par_ref[tile_rows(group, 2 * modes, stride), :]
    skip_sum = jnp.zeros((ROWS, LANES), jnp.float32)

    for first in range(0, modes, HALF):
        lam = [jnp.exp(-par_ref[tile_rows(group, first + m, stride), :]) for m in range(HALF)]
        res = [par_ref[tile_rows(group, modes + first + m, stride), :] for m in range(HALF)]
        start = tuple(in_ref[(first + m) // share, (first + m) % share] for m in range(HALF))
        for m in range(HALF):
            states[0, m] = start[m]

        def forward(b, carry, masked):
            x, sums, skips = list(carry[0]), list(carry[1]), carry[2]
            for j in range(STEP):
                t = b * STEP + j
                here = pl.ds(t, ROWS, stride=pitch)
                d = drive[here, :]
                p = pull[here, :]
                if first == 0:
                    total = skip * d
                    skips = skips + p * d
                else:
                    total = filt[here, :]
                for m in range(HALF):
                    if masked:
                        x[m] = lam[m] * keep(t) * x[m] + d
                    else:
                        x[m] = lam[m] * x[m] + d
                    states[t + 1, m] = x[m]
                    sums[m] = sums[m] + p * x[m]
                    total = total + res[m] * x[m]
                filt[here, :] = total
            return tuple(x), tuple(sums), skips

        def backward(b, carry, masked):
            inc, sums = list(carry[0]), list(carry[1])
            for j in reversed(range(STEP)):
                t = b * STEP + j
                here = pl.ds(t, ROWS, stride=pitch)
                p = pull[here, :]
                total = skip * p if first == 0 else gdrive[here, :]
                for m in range(HALF):
                    a = p + inc[m]
                    total = total + res[m] * a
                    inc[m] = lam[m] * keep(t) * a if masked else lam[m] * a
                    sums[m] = sums[m] + inc[m] * states[t, m]
                gdrive[here, :] = total
            return tuple(inc), tuple(sums)

        def forward_body(b, carry):
            return lax.cond(
                broken(b), lambda c: forward(b, c, True), lambda c: forward(b, c, False), carry
            )

        def backward_body(i, carry):
            b = blocks - 1 - i
            return lax.cond(
                broken(b), lambda c: backward(b, c, True), lambda c: backward(b, c, False), carry
            )

        zeros = tuple(jnp.zeros((ROWS, LANES), jnp.float32) for _ in range(HALF))
        _, sums, skip_sum = lax.fori_loop(0, blocks, forward_body, (start, zeros, skip_sum))
        for m in range(HALF):
            grad_ref[tile_rows(group, modes + first + m, stride), :] = sums[m]
        incoming = tuple(in_ref[(first + m) // share, share + (first + m) % share] for m in range(HALF))
        _, sums = lax.fori_loop(0, blocks, backward_body, (incoming, zeros))
        for m in range(HALF):
            grad_ref[tile_rows(group, first + m, stride), :] = -res[m] * sums[m]
    grad_ref[tile_rows(group, 2 * modes, stride), :] = skip_sum
    for row in range(2 * modes + 1, WIDTH):
        grad_ref[tile_rows(group, row, stride), :] = jnp.zeros((ROWS, LANES), jnp.float32)

    for i in range(ROWS):
        cols = pl.ds(i * LANES, LANES)
        rows = pl.ds(i * pitch, tokens)
        f = filt[rows, :]
        g = gdrive[rows, :]
        out_ref[:, cols] = (q_ref[:, cols].astype(jnp.float32) * f).astype(jnp.bfloat16)
        gq_ref[:, cols] = (c_ref[:, cols].astype(jnp.float32) * f).astype(jnp.bfloat16)
        gk_ref[:, cols] = (g * v_ref[:, cols].astype(jnp.float32)).astype(jnp.bfloat16)
        gv_ref[:, cols] = (g * k_ref[:, cols].astype(jnp.float32)).astype(jnp.bfloat16)


def join_kernel(lens_ref, par_ref, all_ref, out_ref, *, modes, tokens, stride, share):
    count = all_ref.shape[0]
    mine = lax.axis_index("ctx")
    group = pl.program_id(0)
    for m in range(modes):
        across = jnp.exp(-float(tokens) * par_ref[tile_rows(group, m, stride), :])

        def turn(i, carry):
            state, adjoint = carry
            j = count - 1 - i
            near = across * opening(lens_ref, i * tokens, (i + 1) * tokens - 1) * state + all_ref[i, m // share, m % share]
            far = across * opening(lens_ref, j * tokens, (j + 1) * tokens - 1) * adjoint + all_ref[j, m // share, share + m % share]
            state = jnp.where(i < mine, near, state)
            adjoint = jnp.where(j > mine, far, adjoint)
            return state, adjoint

        zero = jnp.zeros((ROWS, LANES), jnp.float32)
        state, adjoint = lax.fori_loop(0, count, turn, (zero, zero), unroll=8)
        out_ref[m // share, m % share] = state
        out_ref[m // share, share + m % share] = adjoint


def per_device(hyena_q, hyena_k, hyena_v, hyena_cot, doc_lengths, decay_rate, residues, skip_gain):
    tokens, channels = hyena_q.shape[1], hyena_q.shape[2]
    modes, own = decay_rate.shape
    tiles = channels // LANES
    groups = channels // GROUP
    pitch = tokens + PAD
    count = lax.axis_size("ctx")
    planes = lax.axis_size("dp")
    axes = ("dp", "ctx")
    direct = own == LANES and count == ROWS and modes % 2 == 0 and planes == groups
    stride = planes * WIDTH if direct else WIDTH
    share = modes // 2
    tall = 2 * share
    vmem = pl.BlockSpec(memory_space=pltpu.VMEM)
    smem = pl.BlockSpec(memory_space=pltpu.SMEM)

    def remote(collective):
        return pltpu.CompilerParams(
            collective_id=collective, has_side_effects=True, vmem_limit_bytes=VMEM_LIMIT
        )

    if direct:
        params = pl.pallas_call(
            functools.partial(gather_kernel, planes=planes, count=count),
            in_specs=[vmem, vmem, vmem],
            out_specs=vmem,
            out_shape=jax.ShapeDtypeStruct((tiles * WIDTH, LANES), jnp.float32),
            scratch_shapes=[pltpu.SemaphoreType.DMA((planes - 1,))] * 2
            + [pltpu.SemaphoreType.DMA((count // 2 - 1,))] * 2
            + [pltpu.SemaphoreType.DMA((count // 2,))] * 2,
            compiler_params=remote(0),
            name="gather",
        )(decay_rate, residues, skip_gain[None, :])
    else:
        spare = jnp.zeros((WIDTH - 2 * modes - 1, own), jnp.float32)
        packed = jnp.concatenate([decay_rate, residues, skip_gain[None, :], spare], axis=0)
        params = lax.all_gather(packed, axes, axis=1, tiled=True)
        params = params.reshape(WIDTH, tiles, LANES).transpose(1, 0, 2).reshape(tiles * WIDTH, LANES)

    q, k, v, c = hyena_q[0], hyena_k[0], hyena_v[0], hyena_cot[0]

    whole = pl.BlockSpec((tiles * WIDTH, LANES), lambda g: (0, 0))
    block = pl.BlockSpec((tokens, GROUP), lambda g: (0, g))
    wide = pltpu.VMEM((ROWS * pitch, LANES), jnp.float32)
    limit = pltpu.CompilerParams(vmem_limit_bytes=VMEM_LIMIT)

    def rows_of(n):
        return pl.BlockSpec((n // tall, tall, ROWS, LANES), lambda g: (0, 0, g, 0))

    ends = pl.pallas_call(
        functools.partial(ends_kernel, modes=modes, pitch=pitch, stride=stride, share=share),
        grid=(groups,),
        in_specs=[smem, whole, block, block, block, block],
        out_specs=rows_of(2 * modes),
        out_shape=jax.ShapeDtypeStruct((2 * modes // tall, tall, tiles, LANES), jnp.float32),
        scratch_shapes=[wide, wide],
        compiler_params=limit,
        name="ends",
    )(doc_lengths, params, k, v, c, q)
    if direct:
        part = pltpu.VMEM((tall, tiles, LANES), jnp.float32)
        chips = count // 2
        incoming = pl.pallas_call(
            functools.partial(exchange_kernel, planes=planes, count=count, tokens=tokens),
            in_specs=[smem, vmem, vmem],
            out_specs=vmem,
            out_shape=jax.ShapeDtypeStruct(ends.shape, jnp.float32),
            scratch_shapes=[
                part,
                pltpu.VMEM((2, share, tiles, LANES), jnp.float32),
                pltpu.VMEM((chips, share, tiles, LANES), jnp.float32),
                part,
            ]
            + [pltpu.SemaphoreType.DMA((2,))] * 2
            + [pltpu.SemaphoreType.DMA((chips - 1,))] * 2,
            compiler_params=remote(1),
            name="exchange",
        )(doc_lengths, params, ends)
    else:
        everyone = lax.all_gather(ends, "ctx", axis=0)
        incoming = pl.pallas_call(
            functools.partial(join_kernel, modes=modes, tokens=tokens, stride=stride, share=share),
            grid=(groups,),
            in_specs=[
                smem, whole,
                pl.BlockSpec((count, 2 * modes // tall, tall, ROWS, LANES), lambda g: (0, 0, 0, g, 0)),
            ],
            out_specs=rows_of(2 * modes),
            out_shape=jax.ShapeDtypeStruct(ends.shape, jnp.float32),
            compiler_params=limit,
            name="join",
        )(doc_lengths, params, everyone)
    big = jax.ShapeDtypeStruct((tokens, channels), jnp.bfloat16)
    hyena_out, grad_q, grad_k, grad_v, grads = pl.pallas_call(
        functools.partial(main_kernel, modes=modes, pitch=pitch, stride=stride, share=share),
        grid=(groups,),
        in_specs=[smem, whole, rows_of(2 * modes), block, block, block, block],
        out_specs=[block, block, block, block, whole],
        out_shape=[big, big, big, big, jax.ShapeDtypeStruct((tiles * WIDTH, LANES), jnp.float32)],
        scratch_shapes=[wide, wide, wide, wide, pltpu.VMEM((tokens + 1, HALF, ROWS, LANES), jnp.float32)],
        compiler_params=limit,
        name="main",
    )(doc_lengths, params, incoming, k, v, c, q)
    if direct:
        chunk = planes * WIDTH
        row = jax.ShapeDtypeStruct((modes, LANES), jnp.float32)
        grad_rate, grad_residues, grad_skip = pl.pallas_call(
            functools.partial(reduce_kernel, planes=planes, count=count),
            in_specs=[vmem],
            out_specs=[vmem, vmem, vmem],
            out_shape=[row, row, jax.ShapeDtypeStruct((1, LANES), jnp.float32)],
            scratch_shapes=[
                pltpu.VMEM((chips, chunk, LANES), jnp.float32),
                pltpu.VMEM((chips - 1, chunk, LANES), jnp.float32),
                pltpu.VMEM((chips - 1, chunk, LANES), jnp.float32),
                pltpu.VMEM((planes, WIDTH, LANES), jnp.float32),
                pltpu.VMEM((planes - 1, WIDTH, LANES), jnp.float32),
            ]
            + [pltpu.SemaphoreType.DMA((chips,))] * 2
            + [pltpu.SemaphoreType.DMA((chips - 1,))] * 2
            + [pltpu.SemaphoreType.DMA((planes - 1,))] * 2,
            compiler_params=remote(2),
            name="reduce",
        )(grads.reshape(count, chunk, LANES))
        grad_skip = grad_skip[0]
    else:
        grads = grads.reshape(tiles, WIDTH, LANES).transpose(1, 0, 2).reshape(WIDTH, channels)
        shared = lax.psum_scatter(grads, axes, scatter_dimension=1, tiled=True)
        grad_rate, grad_residues, grad_skip = shared[:modes], shared[modes : 2 * modes], shared[2 * modes]
    return (
        hyena_out[None], grad_q[None], grad_k[None], grad_v[None],
        grad_rate, grad_residues, grad_skip,
    )


def solution(mesh):
    tokens_split = P("dp", "ctx", None)
    by_channel = P(None, ("dp", "ctx"))
    return jax.shard_map(
        per_device,
        mesh=mesh,
        in_specs=(tokens_split,) * 4 + (P("dp", None), by_channel, by_channel, P(("dp", "ctx"))),
        out_specs=(tokens_split,) * 4 + (by_channel, by_channel, P(("dp", "ctx"))),
        check_vma=False,
    )
```
